32 devices in a mesh: dp: 4 (over x, core), expert: 8 (over z, y).
Axes of the slice: x: 2, y: 2, z: 4, core: 2. Of those that a mesh axis runs over, the one named last changes fastest.
Arguments:
- hidden_states: bfloat16 [4096, 2880], P(('dp', 'expert')), may hold values from -12 to 12
- route_ids: int32 [4096, 4], P(('dp', 'expert')), may hold values from 0 to 7, all different within a row; in each aligned block of 128 rows (0 to 127, 128 to 255, ...) at most 68 rows name the same one
- route_weights: bfloat16 [4096, 4], P(('dp', 'expert')), may hold values from 0.099609375 to 0.59765625
- gate_up_proj: bfloat16 [8, 1440, 2, 2880], P('expert', 'dp'), may hold values from -0.109375 to 0.109375
- down_proj: bfloat16 [8, 1440, 2880], P('expert', 'dp'), may hold values from -0.15625 to 0.15625
Outputs:
- moe_output: bfloat16 [4096, 2880], P(('dp', 'expert'))
The draws below stay inside these ranges and needn't reach their ends.
Inputs may be any that keep to these rules, and one draw needn't show every extreme that they name: `route_ids`: each token names 4 different experts. Among the tokens of one device (aligned blocks of 128 tokens) no expert is named more than 68 times, and in some block an expert is named exactly 68 times.
All inputs are finite; a program needn't handle non-finite values.
Results may differ from the reference program's by a relative error of at most 0.0057.
Values may be sent and summed in bfloat16 or wider, within the bound.
No kernel may reach another device: no remote copies, remote signals or barrier semaphores. Data moves between devices by JAX's collectives and lax.ppermute only.
A program may use at most 192 MiB of HBM per device.

```python
import math
import jax
import jax.numpy as jnp
import numpy as np
from jax import lax

D = 2880
FF = 1440
TOP = 4
TOK_DEV = 128
EXPERTS = 8
CAP = 68
TOKENS = 4096


def draw_hidden_states(key, part):
    base_key = jax.random.fold_in(key, 11)
    scale_key = jax.random.fold_in(key, 23)
    row_scale = jnp.exp(jax.random.uniform(scale_key, (TOKENS, 1), jnp.float32, math.log(0.5), math.log(3.0)))
    values = jnp.clip(jax.random.normal(base_key, (TOKENS, D), jnp.float32), -4.0, 4.0)
    return (values * row_scale).astype(jnp.bfloat16)


def level_of(key, shape, shards, low, largest):
    level, own = 1.0, jax.random.fold_in(key, 6)
    for dim, parts in shards:
        heights = jnp.exp(jax.random.uniform(jax.random.fold_in(own, dim), (parts,), jnp.float32, low / len(shards), largest / len(shards)))
        level = level * jnp.repeat(heights, shape[dim] // parts).reshape([-1 if axis == dim else 1 for axis in range(len(shape))])
    return level


def assign_block(own_key, own, number, rows, number_of, top, most, skew):
    order = jax.random.permutation(own_key, number_of)
    crowded, common = load_shares(number_of, rows * top, most, skew, True), load_shares(number_of, rows * top, most, skew, False)
    places = jnp.arange(number_of)

    def named(sizes, offset_by):
        used = int((sizes > 0).sum())
        fixed = max(1, used // 4)
        passed = fixed + (places - fixed + offset_by * (used - fixed)) % max(1, number_of - fixed)
        return jnp.zeros((number_of,), jnp.int32).at[order[jnp.where(places < fixed, places, passed)]].set(jnp.asarray(sizes, jnp.int32))

    sizes = jnp.where(number % 4 == 0, named(crowded, number // 4), named(common, number - number // 4 - 1))
    mixed = jax.random.permutation(jax.random.fold_in(own, 3), number_of)
    giver, receiver = mixed[0:number_of // 2 * 2:2], mixed[1:number_of // 2 * 2:2]
    margin = jnp.minimum(sizes[giver] - 1, most - sizes[receiver]) // 2
    margin = jnp.where((giver == order[0]) | (receiver == order[0]) | (sizes[receiver] == 0), 0, jnp.maximum(margin, 0))
    passed = jax.random.randint(jax.random.fold_in(own, 4), (number_of // 2,), 0, 1 << 20) % (margin + 1)
    sizes = sizes.at[giver].add(-passed).at[receiver].add(passed)
    labels = jnp.searchsorted(jnp.cumsum(sizes), jnp.arange(rows * top), side="right").astype(jnp.int32)
    table = labels.reshape(top, rows).T
    table = table[jax.random.permutation(jax.random.fold_in(own, 1), rows)]
    offset_by = jax.random.randint(jax.random.fold_in(own, 2), (rows, 1), 0, top)
    return jnp.take_along_axis(table, (jnp.arange(top)[None, :] + offset_by) % top, axis=1)


def load_shares(count, total, limit, skew, full):
    portions = [(1 << 20) // math.isqrt(grade ** skew) + 1 for grade in range(1, count + 1)]
    largest = limit if full else min(limit, max(-(-total // count), total * portions[0] // sum(portions)))
    least = 1 if total - largest >= count - 1 else 0
    counts, spare = [largest] + [least] * (count - 1), total - largest - least * (count - 1)
    while spare > 0:
        movable = [i for i in range(1, count) if counts[i] < largest] or [i for i in range(1, count) if counts[i] < limit]
        pool, left = sum([portions[i] for i in movable]), spare
        for i in movable:
            extra = min(limit - counts[i], max(1, left * portions[i] // pool), spare)
            counts[i] = counts[i] + extra
            spare = spare - extra
    return np.array(counts)


def noise(key, dims, scale, most, shards=(), held_as=jnp.bfloat16):
    drawn = jax.random.normal(key, dims, jnp.float32) * scale
    if len(shards) > 0:
        drawn = level_of(key, dims, shards, -0.22, 0.18) * drawn
    return jnp.clip(drawn, min=-most, max=most).astype(held_as)


def setup_inputs(seed: int = 0) -> dict:
    seeds = jax.random.split(jax.random.key(seed), 6)
    hidden_states = draw_hidden_states(jax.random.fold_in(seeds[5], 71), 0)
    route_ids_keys = jax.random.split(jax.random.fold_in(seeds[1], 1), TOKENS // TOK_DEV)
    route_ids_turns = jax.random.permutation(jax.random.fold_in(seeds[1], 3), TOKENS // TOK_DEV)
    route_ids = jax.vmap(lambda own, number: assign_block(jax.random.fold_in(seeds[1], 2), own, number, TOK_DEV, EXPERTS, TOP, CAP, 1))(route_ids_keys, route_ids_turns).reshape((TOKENS, TOP))
    route_weights = jnp.clip(0.099609375 + 0.49804688 * jax.random.uniform(seeds[2], (TOKENS, TOP), jnp.float32) ** level_of(seeds[2], (TOKENS, TOP), ((0, 32),), -0.2, 0.2), 0.099609375, 0.59765625).astype(jnp.bfloat16)
    gate_up_proj = noise(seeds[3], (EXPERTS, FF, 2, D), D ** -0.5, 0.109375, ((0, 8), (1, 4)))
    down_proj = noise(seeds[4], (EXPERTS, FF, D), FF ** -0.5, 0.15625, ((0, 8), (1, 4)))
    return dict(hidden_states=hidden_states, route_ids=route_ids, route_weights=route_weights, gate_up_proj=gate_up_proj, down_proj=down_proj)


clamp_limit = 7.0


def reference(hidden_states, route_ids, route_weights, gate_up_proj, down_proj):
    blocks = TOKENS // TOK_DEV
    routes = TOK_DEV * TOP
    block_ids = route_ids.reshape(blocks, routes).astype(jnp.int32)
    position = jnp.arange(routes, dtype=jnp.int32)

    def block_rank(ids_row):
        earlier = (ids_row[:, None] == ids_row[None, :]) & (position[None, :] < position[:, None])
        return jnp.sum(earlier.astype(jnp.int32), axis=1).astype(jnp.int32)

    rank_in = lax.map(block_rank, block_ids)
    block_index = jnp.broadcast_to(jnp.arange(blocks, dtype=jnp.int32)[:, None], (blocks, routes))
    token_index = (block_index * TOK_DEV + position[None, :] // TOP).astype(jnp.int32)
    slot_token = jnp.full((EXPERTS, blocks, CAP), TOKENS, jnp.int32).at[block_ids, block_index, rank_in].set(token_index)
    slot_weight = jnp.zeros((EXPERTS, blocks, CAP), jnp.float32).at[block_ids, block_index, rank_in].set(
        route_weights.reshape(blocks, routes).astype(jnp.float32))
    padded = jnp.concatenate([hidden_states, jnp.zeros((1, D), jnp.bfloat16)], axis=0)

    def one_expert(running_sum, inputs):
        gate_up, down, tokens_at, weights_at = inputs
        token_list = tokens_at.reshape(blocks * CAP)
        token_rows = padded[token_list]
        gate_values = jnp.dot(token_rows, gate_up[:, 0, :].T, preferred_element_type=jnp.float32)
        upper_values = jnp.dot(token_rows, gate_up[:, 1, :].T, preferred_element_type=jnp.float32)
        gate_values = jnp.minimum(gate_values, clamp_limit)
        upper_values = jnp.clip(upper_values, -clamp_limit, clamp_limit)
        hidden = ((upper_values + 1.0) * gate_values * jax.nn.sigmoid(1.702 * gate_values)).astype(jnp.bfloat16)
        expert_out = jnp.dot(hidden, down, preferred_element_type=jnp.float32)
        expert_out = lax.optimization_barrier(expert_out.astype(jnp.bfloat16)).astype(jnp.float32)
        weighted = expert_out * weights_at.reshape(blocks * CAP)[:, None]
        running_sum = running_sum.at[token_list].add(weighted, mode="drop")
        return running_sum, None

    running_sum, unused = lax.scan(one_expert, jnp.zeros((TOKENS, D), jnp.float32),
                                   (gate_up_proj, down_proj, slot_token, slot_weight))
    return running_sum.astype(jnp.bfloat16)
```

```python
import functools

import jax
import jax.numpy as jnp
from jax import lax
from jax.experimental import pallas as pl
from jax.experimental.pallas import tpu as pltpu
from jax.sharding import PartitionSpec as P

clamp_limit = 7.0
AXES = ("dp", "expert")
VMEM_LIMIT = 40 * 1024 * 1024


def chunk_bounds(total, parts, unit):
    step = -(-total // (parts * unit)) * unit
    return [(low, min(low + step, total)) for low in range(0, total, step)]


def sent_to(array, target):
    dp_size, expert_size = lax.axis_size("dp"), lax.axis_size("expert")
    pairs = []
    for d in range(dp_size):
        for e in range(expert_size):
            td, te = target(d, e)
            pairs.append((d * expert_size + e, td * expert_size + te))
    return lax.ppermute(array, AXES, pairs)


def to_other_core(array):
    return sent_to(array, lambda d, e: (d ^ 1, e))


def to_chip(array, step):
    dp_size = lax.axis_size("dp")
    return sent_to(array, lambda d, e: ((d + 2 * step) % dp_size, e))


def to_expert(array, offset):
    return sent_to(array, lambda d, e: (d, e ^ offset))


def call_kernel(body, out_shapes, args, flops):
    moved = sum(a.size * a.dtype.itemsize for a in args) + sum(s.size * s.dtype.itemsize for s in out_shapes)
    return pl.pallas_call(
        body,
        out_shape=out_shapes,
        in_specs=[pl.BlockSpec(memory_space=pltpu.VMEM)] * len(args),
        out_specs=[pl.BlockSpec(memory_space=pltpu.VMEM)] * len(out_shapes),
        compiler_params=pltpu.CompilerParams(vmem_limit_bytes=VMEM_LIMIT),
        cost_estimate=pl.CostEstimate(flops=flops, bytes_accessed=moved, transcendentals=0),
    )(*args)


def pick_kernel(groups, sel_ref, hid_ref, *out_refs):
    hid = hid_ref[...]
    for k in range(groups):
        out_refs[k][...] = jnp.dot(sel_ref[k], hid, preferred_element_type=jnp.float32).astype(jnp.bfloat16)


def down_kernel(shards, *refs):
    hidden_refs, weight_refs, out_refs = refs[:shards], refs[shards : 2 * shards], refs[2 * shards :]
    total = jnp.dot(hidden_refs[0][...], weight_refs[0][...], preferred_element_type=jnp.float32)
    for s in range(1, shards):
        total += jnp.dot(hidden_refs[s][...], weight_refs[s][...], preferred_element_type=jnp.float32)
    rows = total.shape[0] // len(out_refs)
    for k, out_ref in enumerate(out_refs):
        out_ref[...] = total[k * rows : (k + 1) * rows].astype(jnp.bfloat16)


def combine_kernel(groups, table_ref, *refs):
    total = jnp.dot(table_ref[0], refs[0][...], preferred_element_type=jnp.float32)
    for k in range(1, groups):
        total += jnp.dot(table_ref[k], refs[k][...], preferred_element_type=jnp.float32)
    refs[groups][...] = total.astype(jnp.bfloat16)


def glu(rows, weights):
    gate = lax.dot_general(rows, weights[0], (((1,), (1,)), ((), ())), preferred_element_type=jnp.float32)
    upper = lax.dot_general(rows, weights[1], (((1,), (1,)), ((), ())), preferred_element_type=jnp.float32)
    gate = jnp.minimum(gate, clamp_limit)
    upper = jnp.clip(upper, -clamp_limit, clamp_limit)
    return ((upper + 1.0) * gate * jax.nn.sigmoid(1.702 * gate)).astype(jnp.bfloat16)


def local(hidden_states, route_ids, route_weights, gate_up_proj, down_proj):
    tok_rows, width = hidden_states.shape
    top_count = route_ids.shape[1]
    units = gate_up_proj.shape[1]
    groups = lax.axis_size("expert")
    chips = lax.axis_size("dp") // 2
    capacity = max(2, 17 * tok_rows * top_count // (16 * groups))
    slots = -(-capacity // 8) * 8
    me = lax.axis_index("expert")

    pieces = [(0, 2 * units // 3 // 8 * 8), (2 * units // 3 // 8 * 8, units)]
    own_gu = [jnp.transpose(gate_up_proj[0, a:b], (1, 0, 2)) for a, b in pieces]
    chunks = chunk_bounds(width, 4, 128)
    own_dn = [down_proj[0, :, a:b] for a, b in chunks]
    far_gu = [[to_chip(p, s) for p in own_gu] for s in range(1, chips)]
    far_dn = [[to_chip(c, s) for c in own_dn] for s in range(1, chips)]
    gu = [own_gu, [to_other_core(p) for p in own_gu]]
    dn = [own_dn, [to_other_core(c) for c in own_dn]]
    for s in range(chips - 1):
        gu += [far_gu[s], [to_other_core(p) for p in far_gu[s]]]
        dn += [far_dn[s], [to_other_core(c) for c in far_dn[s]]]

    near = (route_ids ^ me)[:, :, None] == jnp.arange(groups, dtype=jnp.int32)
    member = jnp.any(near, axis=1)
    weight = jnp.sum(jnp.where(near, route_weights[:, :, None].astype(jnp.float32), 0.0), axis=1)
    before = jnp.tril(jnp.ones((tok_rows, tok_rows), jnp.bfloat16), -1)
    rank = jnp.dot(before, member.astype(jnp.bfloat16), preferred_element_type=jnp.float32).astype(jnp.int32)
    rank = jnp.where(member, rank, -1)
    chosen = rank.T[:, None, :] == jnp.arange(slots, dtype=jnp.int32)[None, :, None]
    table = jnp.where(rank.T[:, :, None] == jnp.arange(slots, dtype=jnp.int32), weight.T[:, :, None], 0.0)
    table = table.astype(jnp.bfloat16)

    outgoing = call_kernel(
        functools.partial(pick_kernel, groups),
        [jax.ShapeDtypeStruct((slots, width), jnp.bfloat16)] * groups,
        (chosen.astype(jnp.bfloat16), hidden_states),
        2 * groups * slots * tok_rows * width,
    )
    arrived = [outgoing[0]] + [to_expert(outgoing[k], k) for k in range(1, groups)]
    rows = jnp.concatenate(arrived, axis=0)

    hidden = [jnp.concatenate([glu(rows, p) for p in shard], axis=1) for shard in gu]
    results = []
    for j, (a, b) in enumerate(chunks):
        outs = call_kernel(
            functools.partial(down_kernel, len(dn)),
            [jax.ShapeDtypeStruct((slots, b - a), jnp.bfloat16)] * groups,
            (*hidden, *[shard[j] for shard in dn]),
            2 * groups * slots * units * len(dn) * (b - a),
        )
        returned = [outs[0]] + [to_expert(outs[k], k) for k in range(1, groups)]
        results += call_kernel(
            functools.partial(combine_kernel, groups),
            [jax.ShapeDtypeStruct((tok_rows, b - a), jnp.bfloat16)],
            (table, *returned),
            2 * groups * slots * tok_rows * (b - a),
        )
    return jnp.concatenate(results, axis=1)


def solution(mesh):
    placed = (
        P(("dp", "expert"), None),
        P(("dp", "expert"), None),
        P(("dp", "expert"), None),
        P("expert", "dp", None, None),
        P("expert", "dp", None),
    )
    return jax.shard_map(
        local, mesh=mesh, in_specs=placed, out_specs=P(("dp", "expert"), None), check_vma=False
    )
```

```python
import functools

import jax
import jax.numpy as jnp
from jax import lax
from jax.experimental import pallas as pl
from jax.experimental.pallas import tpu as pltpu
from jax.sharding import PartitionSpec as P

clamp_limit = 7.0
AXES = ("dp", "expert")
VMEM_LIMIT = 12 * 1024 * 1024
FAR_IN = 3
TIES = {11: (7,), 13: (6,), 14: (5,), 15: (4,)}
F32, BF16 = jnp.float32, jnp.bfloat16


def sent_to(array, target):
    dp_size, expert_size = lax.axis_size("dp"), lax.axis_size("expert")
    pairs = []
    for d in range(dp_size):
        for e in range(expert_size):
            td, te = target(d, e)
            pairs.append((d * expert_size + e, td * expert_size + te))
    return lax.ppermute(array, AXES, pairs)


def to_other_core(array):
    return sent_to(array, lambda d, e: (d ^ 1, e))


def to_chip(step):
    dp_size = lax.axis_size("dp")
    return lambda array: sent_to(array, lambda d, e: ((d + 2 * step) % dp_size, e))


def to_expert(offset):
    return lambda array: sent_to(array, lambda d, e: (d, e ^ offset))


def after(array, *others):
    return lax.optimization_barrier((array, others))[0]


class Line:
    def __init__(self, depth):
        self.depth = depth
        self.done = []

    def send(self, array, move, ties=()):
        if len(self.done) >= self.depth:
            ties = [*ties, self.done[-self.depth]]
        if ties:
            array = after(array, *ties)
        moved = move(array)
        self.done.append(moved)
        return moved


def call_kernel(body, out_shapes, args, flops):
    moved = sum(a.size * a.dtype.itemsize for a in args) + sum(s.size * s.dtype.itemsize for s in out_shapes)
    return pl.pallas_call(
        body,
        out_shape=out_shapes,
        in_specs=[pl.BlockSpec(memory_space=pltpu.VMEM)] * len(args),
        out_specs=[pl.BlockSpec(memory_space=pltpu.VMEM)] * len(out_shapes),
        compiler_params=pltpu.CompilerParams(vmem_limit_bytes=VMEM_LIMIT),
        cost_estimate=pl.CostEstimate(flops=flops, bytes_accessed=moved, transcendentals=0),
    )(*args)


def pick_kernel(sel_ref, hid_ref, *out_refs):
    hid = hid_ref[...]
    for k, out_ref in enumerate(out_refs):
        out_ref[...] = jnp.dot(sel_ref[k], hid, preferred_element_type=F32).astype(BF16)


def expert_kernel(blocks, shards, *refs):
    row_refs, up_refs, down_refs = refs[:blocks], refs[blocks : blocks + shards], refs[blocks + shards : blocks + 2 * shards]
    out_refs = refs[blocks + 2 * shards :]
    rows = jnp.concatenate([ref[...].astype(F32) for ref in row_refs], axis=0).astype(BF16)
    dims = (((1,), (1,)), ((), ()))
    total = None
    for up_ref, down_ref in zip(up_refs, down_refs):
        gate = lax.dot_general(rows, up_ref[0], dims, preferred_element_type=F32)
        upper = lax.dot_general(rows, up_ref[1], dims, preferred_element_type=F32)
        gate = jnp.minimum(gate, clamp_limit)
        upper = jnp.clip(upper, -clamp_limit, clamp_limit)
        hidden = ((upper + 1.0) * gate * jax.nn.sigmoid(1.702 * gate)).astype(BF16)
        part = jnp.dot(hidden, down_ref[...], preferred_element_type=F32)
        total = part if total is None else total + part
    slots = total.shape[0] // blocks
    for s, out_ref in enumerate(out_refs):
        out_ref[...] = total[s * slots : (s + 1) * slots].astype(out_ref.dtype)


def add_kernel(*refs):
    total = refs[0][...]
    for ref in refs[1:-1]:
        total += ref[...].astype(F32)
    refs[-1][...] = total.astype(BF16)


def combine_kernel(table_ref, *refs):
    total = jnp.dot(table_ref[0], refs[0][...], preferred_element_type=F32)
    for k in range(1, len(refs) - 1):
        total += jnp.dot(table_ref[k], refs[k][...], preferred_element_type=F32)
    refs[-1][...] = total.astype(BF16)


def plan(groups):
    half = groups // 2
    far, near = list(range(groups - 1, half - 1, -1)), list(range(2, half))
    steps = [("out", 0), ("out", 1), ("out", far[0]), ("back", 1)]
    for last, k in zip(far, far[1:]):
        steps += [("out", k), ("back", last)]
    steps += [("back", far[-1])]
    steps += [("out", k) for k in near] + [("back", k) for k in near] + [("back", 0)]
    return steps


def local(hidden_states, route_ids, route_weights, gate_up_proj, down_proj):
    tok_rows, width = hidden_states.shape
    top_count = route_ids.shape[1]
    units = gate_up_proj.shape[1]
    groups = lax.axis_size("expert")
    chips = lax.axis_size("dp") // 2
    capacity = max(2, 17 * tok_rows * top_count // (16 * groups))
    slots = -(-capacity // 8) * 8
    half = groups // 2
    me = lax.axis_index("expert")

    near = (route_ids ^ me)[:, :, None] == jnp.arange(groups, dtype=jnp.int32)
    member = jnp.any(near, axis=1)
    weight = jnp.sum(jnp.where(near, route_weights[:, :, None].astype(F32), 0.0), axis=1)
    before = jnp.tril(jnp.ones((tok_rows, tok_rows), BF16), -1)
    rank = jnp.dot(before, member.astype(BF16), preferred_element_type=F32).astype(jnp.int32)
    rank = jnp.where(member, rank, -1)
    slot_range = jnp.arange(slots, dtype=jnp.int32)
    chosen = rank.T[:, None, :] == slot_range[None, :, None]
    table = jnp.where(rank.T[:, :, None] == slot_range, weight.T[:, :, None], 0.0).astype(BF16)
    outgoing = call_kernel(
        pick_kernel,
        [jax.ShapeDtypeStruct((slots, width), BF16)] * groups,
        (chosen.astype(BF16), hidden_states),
        2 * groups * slots * tok_rows * width,
    )

    between_chips = Line(2 * (chips - 1))
    far_in, near_in, far_out, near_out = Line(FAR_IN), Line(1), Line(2), Line(1)
    rows = [outgoing[0]] + [None] * (groups - 1)
    for k in range(groups - 1, half - 1, -1):
        rows[k] = far_in.send(outgoing[k], to_expert(k))
    rows[1] = near_in.send(outgoing[1], to_expert(1))

    weights, partial, results = [], {}, [None] * groups
    steps = plan(groups)
    for number, (what, k) in enumerate(steps):
        ties = [results[t] for t in TIES.get(number, ()) if t < groups and results[t] is not None]
        if what == "out":
            if k >= 2 and k < half:
                rows[k] = near_in.send(rows[k], to_expert(k))
            others = [between_chips.send(rows[k], to_chip(s), ties) for s in range(1, chips)]
            if k == 0:
                own_gu = jnp.transpose(after(gate_up_proj[0], *others), (1, 0, 2))
                core_gu = to_other_core(own_gu)
                core_dn = to_other_core(after(down_proj[0], *others))
                weights = [own_gu, core_gu, down_proj[0], core_dn]
                near_in.done.append(core_dn)
                for t in range(2, half):
                    rows[t] = outgoing[t]
            partial[k] = call_kernel(
                functools.partial(expert_kernel, chips, 2),
                [jax.ShapeDtypeStruct((slots, width), F32)] + [jax.ShapeDtypeStruct((slots, width), BF16)] * (chips - 1),
                (rows[k], *others, *weights),
                6 * chips * slots * width * 2 * units,
            )
            continue
        mine, *foreign = partial[k]
        back = [between_chips.send(v, to_chip(-s), ties) for s, v in enumerate(foreign, 1)]
        out, = call_kernel(add_kernel, [jax.ShapeDtypeStruct((slots, width), BF16)], (mine, *back), 0)
        line = far_out if k >= half else near_out
        results[k] = line.send(out, to_expert(k)) if k else out
    combined, = call_kernel(
        combine_kernel,
        [jax.ShapeDtypeStruct((tok_rows, width), BF16)],
        (table, *results),
        2 * groups * slots * tok_rows * width,
    )
    return combined


def solution(mesh):
    placed = (
        P(("dp", "expert"), None),
        P(("dp", "expert"), None),
        P(("dp", "expert"), None),
        P("expert", "dp", None, None),
        P("expert", "dp", None),
    )
    return jax.shard_map(
        local, mesh=mesh, in_specs=placed, out_specs=P(("dp", "expert"), None), check_vma=False
    )
```

```python
import functools

import jax
import jax.numpy as jnp
from jax import lax
from jax.experimental import pallas as pl
from jax.experimental.pallas import tpu as pltpu
from jax.sharding import PartitionSpec as P

clamp_limit = 7.0
AXES = ("dp", "expert")
VMEM_LIMIT = 12 * 1024 * 1024
F32, BF16 = jnp.float32, jnp.bfloat16
PARAMS = {'far': [4, 2, 5, 6, 3, 7],
 'far_in': 3,
 'far_out': 2,
 'kcost': 6,
 'late': 2,
 'near_in': 1,
 'plan': [('out', 0),
          ('out', 1),
          ('out', 4),
          ('out', 2),
          ('back', 4),
          ('out', 6),
          ('back', 2),
          ('out', 5),
          ('back', 5),
          ('out', 3),
          ('back', 6),
          ('out', 7),
          ('back', 3),
          ('back', 7),
          ('back', 1),
          ('back', 0)],
 'ties': {'dn': (('out', 0), ('z', 1), ('z', 4)),
          'gu': (('out', 0), ('z', 1), ('z', 4)),
          ('back', 0): (('r', 3),),
          ('back', 1): (('r', 6),),
          ('back', 3): (('r', 5),),
          ('back', 7): (('r', 2),),
          ('out', 3): (('r', 4),),
          ('z', 3): (('r', 7),)},
 'xdepth': 3}


def sent_to(array, target):
    dp_size, expert_size = lax.axis_size("dp"), lax.axis_size("expert")
    pairs = []
    for d in range(dp_size):
        for e in range(expert_size):
            td, te = target(d, e)
            pairs.append((d * expert_size + e, td * expert_size + te))
    return lax.ppermute(array, AXES, pairs)


def to_other_core(array):
    return sent_to(array, lambda d, e: (d ^ 1, e))


def to_chip(step):
    dp_size = lax.axis_size("dp")
    return lambda array: sent_to(array, lambda d, e: ((d + 2 * step) % dp_size, e))


def moved(e, k, groups, sign):
    return (e // 2 + sign * (k // 2)) % (groups // 2) * 2 + (e % 2 ^ k % 2)


def to_expert(k):
    return lambda array: sent_to(array, lambda d, e: (d, moved(e, k, lax.axis_size("expert"), 1)))


def from_expert(k):
    return lambda array: sent_to(array, lambda d, e: (d, moved(e, k, lax.axis_size("expert"), -1)))


def after(array, *others):
    return lax.optimization_barrier((array, others))[0] if others else array


class Line:
    def __init__(self, depth):
        self.depth = depth
        self.done = []

    def send(self, array, move, ties=()):
        if len(self.done) >= self.depth:
            ties = [*ties, self.done[-self.depth]]
        moved = move(after(array, *ties))
        self.done.append(moved)
        return moved


def call_kernel(body, out_shapes, args, flops, scratch=()):
    moved = sum(a.size * a.dtype.itemsize for a in args) + sum(s.size * s.dtype.itemsize for s in out_shapes)
    return pl.pallas_call(
        body,
        out_shape=out_shapes,
        in_specs=[pl.BlockSpec(memory_space=pltpu.VMEM)] * len(args),
        out_specs=[pl.BlockSpec(memory_space=pltpu.VMEM)] * len(out_shapes),
        scratch_shapes=[pltpu.VMEM(shape, F32) for shape in scratch],
        compiler_params=pltpu.CompilerParams(vmem_limit_bytes=VMEM_LIMIT),
        cost_estimate=pl.CostEstimate(flops=flops, bytes_accessed=moved, transcendentals=0),
    )(*args)


def packed_rows(capacity, width):
    tiles, rest = divmod(width, 128)
    assert rest * 2 <= 128
    first = -(-(-(-capacity // 2)) // 8) * 8
    return -(-(tiles * capacity + (first if rest else 0)) // 16) * 16, first


def pack(block, capacity, out_ref):
    rows, width = block.shape
    tiles, rest = divmod(width, 128)
    for t in range(tiles):
        out_ref[pl.ds(t * capacity, rows)] = block[:, t * 128 : (t + 1) * 128]
    if rest:
        first = packed_rows(capacity, width)[1]
        left, right = block[:first, tiles * 128 :], block[first:, tiles * 128 :]
        if rows - first < first:
            right = jnp.concatenate([right, jnp.zeros((2 * first - rows, rest), F32)], axis=0)
        parts = [left, right[:first]]
        if rest < 64:
            parts = [jnp.pad(p, ((0, 0), (0, 64 - rest))) for p in parts]
        out_ref[pl.ds(tiles * capacity, first)] = jnp.concatenate(parts, axis=1)


def unpack(packed_ref, capacity, rows, low, out_ref):
    width = out_ref.shape[1]
    tiles, rest = divmod(width, 128)
    for t in range(tiles):
        out_ref[low : low + rows, t * 128 : (t + 1) * 128] = packed_ref[pl.ds(t * capacity, rows)]
    if rest:
        first = packed_rows(capacity, width)[1]
        tail = packed_ref[pl.ds(tiles * capacity, first)]
        out_ref[low : low + first, tiles * 128 :] = tail[:, :rest]
        out_ref[low + first : low + rows, tiles * 128 :] = tail[: rows - first, 64 : 64 + rest]


def pick_kernel(capacity, sel_ref, hid_ref, *refs):
    hid, scratch = hid_ref[...].T, refs[-1]
    for k, out_ref in enumerate(refs[:-1]):
        pack(jnp.dot(sel_ref[k], hid, preferred_element_type=F32), capacity, scratch)
        out_ref[...] = scratch[: out_ref.shape[0]].astype(BF16)


def expert_kernel(capacity, blocks, shards, *refs):
    row_refs, up_refs, down_refs = refs[:blocks], refs[blocks : blocks + shards], refs[blocks + shards : blocks + 2 * shards]
    out_refs, packed, spread = refs[blocks + 2 * shards : -2], refs[-2], refs[-1]
    slots = spread.shape[0] // blocks
    for s, ref in enumerate(row_refs):
        packed[: ref.shape[0]] = ref[...].astype(F32)
        unpack(packed, capacity, slots, s * slots, spread)
    rows = spread[...].astype(BF16)
    dims = (((1,), (1,)), ((), ()))
    total = None
    for up_ref, down_ref in zip(up_refs, down_refs):
        gate = lax.dot_general(rows, up_ref[0], dims, preferred_element_type=F32)
        upper = lax.dot_general(rows, up_ref[1], dims, preferred_element_type=F32)
        gate = jnp.minimum(gate, clamp_limit)
        upper = jnp.clip(upper, -clamp_limit, clamp_limit)
        hidden = ((upper + 1.0) * gate * jax.nn.sigmoid(1.702 * gate)).astype(BF16)
        part = jnp.dot(hidden, down_ref[...], preferred_element_type=F32)
        total = part if total is None else total + part
    for s, out_ref in enumerate(out_refs):
        pack(total[s * slots : (s + 1) * slots], capacity, packed)
        out_ref[...] = packed[: out_ref.shape[0]].astype(out_ref.dtype)


def add_kernel(*refs):
    total = refs[0][...]
    for ref in refs[1:-1]:
        total += ref[...].astype(F32)
    refs[-1][...] = total.astype(BF16)


def combine_kernel(capacity, final, blocks, table_ref, *refs):
    out_ref, packed, spread = refs[-3:]
    total = None
    for k in range(blocks):
        packed[: refs[k].shape[0]] = refs[k][...].astype(F32)
        unpack(packed, capacity, spread.shape[0], 0, spread)
        part = jnp.dot(table_ref[k], spread[...].astype(BF16), preferred_element_type=F32)
        total = part if total is None else total + part
    for ref in refs[blocks:-3]:
        total += ref[...]
    out_ref[...] = total.T.astype(BF16) if final else total


def general_plan(groups):
    return [step for k in range(groups) for step in (("out", k), ("back", k))]


def local(hidden_states, route_ids, route_weights, gate_up_proj, down_proj):
    tok_rows, width = hidden_states.shape
    top_count = route_ids.shape[1]
    units = gate_up_proj.shape[1]
    groups = lax.axis_size("expert")
    chips = lax.axis_size("dp") // 2
    capacity = max(2, 17 * tok_rows * top_count // (16 * groups))
    slots = -(-capacity // 8) * 8
    packed = (packed_rows(capacity, width)[0], 128)
    packed_scratch = (packed[0] + slots, 128)
    half = groups // 2
    me = lax.axis_index("expert")
    known = groups == 8 and chips == 2
    steps = PARAMS["plan"] if known else general_plan(groups)
    tied = PARAMS["ties"] if known else {}
    far_order = PARAMS["far"] if known else list(range(2, groups))

    relative = lax.rem(route_ids // 2 - me // 2 + half, half) * 2 + ((route_ids ^ me) & 1)
    near = relative[:, :, None] == jnp.arange(groups, dtype=jnp.int32)
    member = jnp.any(near, axis=1)
    weight = jnp.sum(jnp.where(near, route_weights[:, :, None].astype(F32), 0.0), axis=1)
    before = jnp.tril(jnp.ones((tok_rows, tok_rows), BF16), -1)
    rank = jnp.dot(before, member.astype(BF16), preferred_element_type=F32).astype(jnp.int32)
    rank = jnp.where(member, rank, -1)
    slot_range = jnp.arange(slots, dtype=jnp.int32)
    chosen = rank.T[:, None, :] == slot_range[None, :, None]
    table = jnp.where(rank.T[:, :, None] == slot_range, weight.T[:, :, None], 0.0).astype(BF16)
    outgoing = call_kernel(
        functools.partial(pick_kernel, capacity),
        [jax.ShapeDtypeStruct(packed, BF16)] * groups,
        (chosen.astype(BF16), hidden_states.T),
        2 * groups * slots * tok_rows * width,
        [packed_scratch],
    )

    between_chips, far_in = Line(PARAMS["xdepth"] * (chips - 1)), Line(PARAMS["far_in"])
    near_in, far_out, near_out = Line(PARAMS["near_in"]), Line(PARAMS["far_out"]), Line(1)
    done, rows = {}, [outgoing[0]] + [None] * (groups - 1)

    def ties_of(name):
        return [done[t] for t in tied.get(name, ()) if t in done]

    for k in far_order:
        rows[k] = done["z", k] = far_in.send(outgoing[k], to_expert(k), ties_of(("z", k)))
    rows[1] = done["z", 1] = near_in.send(outgoing[1], to_expert(1), ties_of(("z", 1)))
    partial, results, weights = {}, [None] * groups, None
    for what, k in steps:
        name = (what, k)
        if what == "out":
            if rows[k] is None:
                rows[k] = done["z", k] = near_in.send(outgoing[k], to_expert(k), ties_of(("z", k)))
            others = [between_chips.send(rows[k], to_chip(s), ties_of(name)) for s in range(1, chips)]
            done[name] = others[0]
            if weights is None:
                own_gu = jnp.transpose(after(gate_up_proj[0], *ties_of("copy")), (1, 0, 2))
                core_gu = done["gu"] = to_other_core(after(own_gu, *ties_of("gu")))
                core_dn = done["dn"] = to_other_core(after(down_proj[0], *ties_of("dn")))
                weights = [own_gu, core_gu, down_proj[0], core_dn]
            partial[k] = call_kernel(
                functools.partial(expert_kernel, capacity, chips, 2),
                [jax.ShapeDtypeStruct(packed, F32)] + [jax.ShapeDtypeStruct(packed, BF16)] * (chips - 1),
                (rows[k], *others, *weights),
                PARAMS["kcost"] * chips * slots * width * 2 * units,
                [packed_scratch, (chips * slots, width)],
            )
            continue
        mine, *foreign = partial[k]
        back = [between_chips.send(v, to_chip(-s), ties_of(name)) for s, v in enumerate(foreign, 1)]
        done[name] = back[0]
        out, = call_kernel(add_kernel, [jax.ShapeDtypeStruct(packed, BF16)], (mine, *back), 0)
        line = far_out if k >= 2 else near_out
        results[k] = done["r", k] = line.send(out, from_expert(k), ties_of(("r", k))) if k else out
    order, sums = [k for what, k in steps if what == "back"], ()
    late = min(PARAMS["late"], groups)
    for first, last in ((0, groups - late), (groups - late, groups)):
        blocks, final = order[first:last], last == groups
        if blocks:
            shape = jax.ShapeDtypeStruct((width, tok_rows), BF16) if final else jax.ShapeDtypeStruct((tok_rows, width), F32)
            sums = call_kernel(
                functools.partial(combine_kernel, capacity, final, len(blocks)),
                [shape],
                (jnp.stack([table[k] for k in blocks]), *[results[k] for k in blocks], *sums),
                2 * len(blocks) * slots * tok_rows * width,
                [packed_scratch, (slots, width)],
            )
    return sums[0].T


def solution(mesh):
    placed = (
        P(("dp", "expert"), None),
        P(("dp", "expert"), None),
        P(("dp", "expert"), None),
        P("expert", "dp", None, None),
        P("expert", "dp", None),
    )
    return jax.shard_map(
        local, mesh=mesh, in_specs=placed, out_specs=P(("dp", "expert"), None), check_vma=False
    )
```

```python
import functools

import jax
import jax.numpy as jnp
from jax import lax
from jax.experimental import pallas as pl
from jax.experimental.pallas import tpu as pltpu
from jax.sharding import PartitionSpec as P

clamp_limit = 7.0
AXES = ("dp", "expert")
VMEM_LIMIT = 12 * 1024 * 1024
F32, BF16 = jnp.float32, jnp.bfloat16
PARAMS = {'far': [4, 2, 5, 6, 3, 7],
 'far_in': 3,
 'far_out': 2,
 'kcost': 6,
 'late': 2,
 'near_in': 1,
 'plan': [('out', 0),
          ('out', 1),
          ('out', 4),
          ('out', 2),
          ('back', 4),
          ('out', 6),
          ('back', 2),
          ('out', 5),
          ('back', 5),
          ('out', 3),
          ('out', 7),
          ('back', 6),
          ('back', 7),
          ('back', 3),
          ('back', 1),
          ('back', 0)],
 'ties': {'dn': (('out', 0), ('z', 1), ('z', 4)),
          'gu': (('out', 0), ('z', 1), ('z', 4)),
          ('back', 0): (('r', 3),),
          ('back', 1): (('r', 6),),
          ('back', 3): (('r', 5),),
          ('back', 4): ('dn',),
          ('back', 7): (('r', 2),),
          ('out', 3): (('r', 4),),
          ('z', 3): (('r', 7),)},
 'xdepth': 3}


def sent_to(array, target):
    dp_size, expert_size = lax.axis_size("dp"), lax.axis_size("expert")
    pairs = []
    for d in range(dp_size):
        for e in range(expert_size):
            td, te = target(d, e)
            pairs.append((d * expert_size + e, td * expert_size + te))
    return lax.ppermute(array, AXES, pairs)


def to_other_core(array):
    return sent_to(array, lambda d, e: (d ^ 1, e))


def to_chip(step):
    dp_size = lax.axis_size("dp")
    return lambda array: sent_to(array, lambda d, e: ((d + 2 * step) % dp_size, e))


def moved(e, k, groups, sign):
    return (e // 2 + sign * (k // 2)) % (groups // 2) * 2 + (e % 2 ^ k % 2)


def to_expert(k):
    return lambda array: sent_to(array, lambda d, e: (d, moved(e, k, lax.axis_size("expert"), 1)))


def from_expert(k):
    return lambda array: sent_to(array, lambda d, e: (d, moved(e, k, lax.axis_size("expert"), -1)))


def after(array, *others):
    return lax.optimization_barrier((array, others))[0] if others else array


class Line:
    def __init__(self, depth):
        self.depth = depth
        self.done = []

    def send(self, array, move, ties=()):
        if len(self.done) >= self.depth:
            ties = [*ties, self.done[-self.depth]]
        moved = move(after(array, *ties))
        self.done.append(moved)
        return moved


def call_kernel(body, out_shapes, args, flops, scratch=()):
    moved = sum(a.size * a.dtype.itemsize for a in args) + sum(s.size * s.dtype.itemsize for s in out_shapes)
    return pl.pallas_call(
        body,
        out_shape=out_shapes,
        in_specs=[pl.BlockSpec(memory_space=pltpu.VMEM)] * len(args),
        out_specs=[pl.BlockSpec(memory_space=pltpu.VMEM)] * len(out_shapes),
        scratch_shapes=[pltpu.VMEM(shape, F32) for shape in scratch],
        compiler_params=pltpu.CompilerParams(vmem_limit_bytes=VMEM_LIMIT),
        cost_estimate=pl.CostEstimate(flops=flops, bytes_accessed=moved, transcendentals=0),
    )(*args)


def packed_rows(capacity, width):
    tiles, rest = divmod(width, 128)
    assert rest * 2 <= 128
    first = -(-(-(-capacity // 2)) // 8) * 8
    return -(-(tiles * capacity + (first if rest else 0)) // 16) * 16, first


def pack(block, capacity, out_ref):
    rows, width = block.shape
    tiles, rest = divmod(width, 128)
    for t in range(tiles):
        out_ref[pl.ds(t * capacity, rows)] = block[:, t * 128 : (t + 1) * 128]
    if rest:
        first = packed_rows(capacity, width)[1]
        left, right = block[:first, tiles * 128 :], block[first:, tiles * 128 :]
        if rows - first < first:
            right = jnp.concatenate([right, jnp.zeros((2 * first - rows, rest), F32)], axis=0)
        parts = [left, right[:first]]
        if rest < 64:
            parts = [jnp.pad(p, ((0, 0), (0, 64 - rest))) for p in parts]
        out_ref[pl.ds(tiles * capacity, first)] = jnp.concatenate(parts, axis=1)


def unpack(packed_ref, capacity, rows, low, out_ref):
    width = out_ref.shape[1]
    tiles, rest = divmod(width, 128)
    for t in range(tiles):
        out_ref[low : low + rows, t * 128 : (t + 1) * 128] = packed_ref[pl.ds(t * capacity, rows)]
    if rest:
        first = packed_rows(capacity, width)[1]
        tail = packed_ref[pl.ds(tiles * capacity, first)]
        out_ref[low : low + first, tiles * 128 :] = tail[:, :rest]
        out_ref[low + first : low + rows, tiles * 128 :] = tail[: rows - first, 64 : 64 + rest]


def pick_kernel(capacity, sel_ref, hid_ref, *refs):
    hid, scratch = hid_ref[...].T, refs[-1]
    for k, out_ref in enumerate(refs[:-1]):
        pack(jnp.dot(sel_ref[k], hid, preferred_element_type=F32), capacity, scratch)
        out_ref[...] = scratch[: out_ref.shape[0]].astype(BF16)


def expert_kernel(capacity, blocks, shards, *refs):
    row_refs, up_refs, down_refs = refs[:blocks], refs[blocks : blocks + shards], refs[blocks + shards : blocks + 2 * shards]
    out_refs, packed, spread = refs[blocks + 2 * shards : -2], refs[-2], refs[-1]
    slots = spread.shape[0] // blocks
    for s, ref in enumerate(row_refs):
        packed[: ref.shape[0]] = ref[...].astype(F32)
        unpack(packed, capacity, slots, s * slots, spread)
    rows = spread[...].astype(BF16)
    dims = (((1,), (1,)), ((), ()))
    total = None
    for up_ref, down_ref in zip(up_refs, down_refs):
        gate = lax.dot_general(rows, up_ref[0], dims, preferred_element_type=F32)
        upper = lax.dot_general(rows, up_ref[1], dims, preferred_element_type=F32)
        gate = jnp.minimum(gate, clamp_limit)
        upper = jnp.clip(upper, -clamp_limit, clamp_limit)
        hidden = ((upper + 1.0) * gate * jax.nn.sigmoid(1.702 * gate)).astype(BF16)
        part = jnp.dot(hidden, down_ref[...], preferred_element_type=F32)
        total = part if total is None else total + part
    for s, out_ref in enumerate(out_refs):
        pack(total[s * slots : (s + 1) * slots], capacity, packed)
        out_ref[...] = packed[: out_ref.shape[0]].astype(out_ref.dtype)


def add_kernel(*refs):
    total = refs[0][...]
    for ref in refs[1:-1]:
        total += ref[...].astype(F32)
    refs[-1][...] = total.astype(BF16)


def combine_kernel(capacity, final, blocks, table_ref, *refs):
    out_ref, packed, spread = refs[-3:]
    total = None
    for k in range(blocks):
        packed[: refs[k].shape[0]] = refs[k][...].astype(F32)
        unpack(packed, capacity, spread.shape[0], 0, spread)
        part = jnp.dot(table_ref[k], spread[...].astype(BF16), preferred_element_type=F32)
        total = part if total is None else total + part
    for ref in refs[blocks:-3]:
        total += ref[...]
    out_ref[...] = total.T.astype(BF16) if final else total


def general_plan(groups):
    return [step for k in range(groups) for step in (("out", k), ("back", k))]


def local(hidden_states, route_ids, route_weights, gate_up_proj, down_proj):
    tok_rows, width = hidden_states.shape
    top_count = route_ids.shape[1]
    units = gate_up_proj.shape[1]
    groups = lax.axis_size("expert")
    chips = lax.axis_size("dp") // 2
    capacity = max(2, 17 * tok_rows * top_count // (16 * groups))
    slots = -(-capacity // 8) * 8
    packed = (packed_rows(capacity, width)[0], 128)
    packed_scratch = (packed[0] + slots, 128)
    half = groups // 2
    me = lax.axis_index("expert")
    known = groups == 8 and chips == 2
    steps = PARAMS["plan"] if known else general_plan(groups)
    tied = PARAMS["ties"] if known else {}
    far_order = PARAMS["far"] if known else list(range(2, groups))

    relative = lax.rem(route_ids // 2 - me // 2 + half, half) * 2 + ((route_ids ^ me) & 1)
    near = relative[:, :, None] == jnp.arange(groups, dtype=jnp.int32)
    member = jnp.any(near, axis=1)
    weight = jnp.sum(jnp.where(near, route_weights[:, :, None].astype(F32), 0.0), axis=1)
    before = jnp.tril(jnp.ones((tok_rows, tok_rows), BF16), -1)
    rank = jnp.dot(before, member.astype(BF16), preferred_element_type=F32).astype(jnp.int32)
    rank = jnp.where(member, rank, -1)
    slot_range = jnp.arange(slots, dtype=jnp.int32)
    chosen = rank.T[:, None, :] == slot_range[None, :, None]
    table = jnp.where(rank.T[:, :, None] == slot_range, weight.T[:, :, None], 0.0).astype(BF16)
    outgoing = call_kernel(
        functools.partial(pick_kernel, capacity),
        [jax.ShapeDtypeStruct(packed, BF16)] * groups,
        (chosen.astype(BF16), hidden_states.T),
        2 * groups * slots * tok_rows * width,
        [packed_scratch],
    )

    between_chips, far_in = Line(PARAMS["xdepth"] * (chips - 1)), Line(PARAMS["far_in"])
    near_in, far_out, near_out = Line(PARAMS["near_in"]), Line(PARAMS["far_out"]), Line(1)
    done, rows = {}, [outgoing[0]] + [None] * (groups - 1)

    def ties_of(name):
        return [done[t] for t in tied.get(name, ()) if t in done]

    for k in far_order:
        rows[k] = done["z", k] = far_in.send(outgoing[k], to_expert(k), ties_of(("z", k)))
    rows[1] = done["z", 1] = near_in.send(outgoing[1], to_expert(1), ties_of(("z", 1)))
    partial, results, weights = {}, [None] * groups, None
    for what, k in steps:
        name = (what, k)
        if what == "out":
            if rows[k] is None:
                rows[k] = done["z", k] = near_in.send(outgoing[k], to_expert(k), ties_of(("z", k)))
            others = [between_chips.send(rows[k], to_chip(s), ties_of(name)) for s in range(1, chips)]
            done[name] = others[0]
            if weights is None:
                own_gu = jnp.transpose(after(gate_up_proj[0], *ties_of("copy")), (1, 0, 2))
                core_gu = done["gu"] = to_other_core(after(own_gu, *ties_of("gu")))
                core_dn = done["dn"] = to_other_core(after(down_proj[0], *ties_of("dn")))
                weights = [own_gu, core_gu, down_proj[0], core_dn]
            partial[k] = call_kernel(
                functools.partial(expert_kernel, capacity, chips, 2),
                [jax.ShapeDtypeStruct(packed, F32)] + [jax.ShapeDtypeStruct(packed, BF16)] * (chips - 1),
                (rows[k], *others, *weights),
                PARAMS["kcost"] * chips * slots * width * 2 * units,
                [packed_scratch, (chips * slots, width)],
            )
            continue
        mine, *foreign = partial[k]
        back = [between_chips.send(v, to_chip(-s), ties_of(name)) for s, v in enumerate(foreign, 1)]
        done[name] = back[0]
        out, = call_kernel(add_kernel, [jax.ShapeDtypeStruct(packed, BF16)], (mine, *back), 0)
        line = far_out if k >= 2 else near_out
        results[k] = done["r", k] = line.send(out, from_expert(k), ties_of(("r", k))) if k else out
    order, sums = [k for what, k in steps if what == "back"], ()
    late = min(PARAMS["late"], groups)
    for first, last in ((0, groups - late), (groups - late, groups)):
        blocks, final = order[first:last], last == groups
        if blocks:
            shape = jax.ShapeDtypeStruct((width, tok_rows), BF16) if final else jax.ShapeDtypeStruct((tok_rows, width), F32)
            sums = call_kernel(
                functools.partial(combine_kernel, capacity, final, len(blocks)),
                [shape],
                (jnp.stack([table[k] for k in blocks]), *[results[k] for k in blocks], *sums),
                2 * len(blocks) * slots * tok_rows * width,
                [packed_scratch, (slots, width)],
            )
    return sums[0].T


def solution(mesh):
    placed = (
        P(("dp", "expert"), None),
        P(("dp", "expert"), None),
        P(("dp", "expert"), None),
        P("expert", "dp", None, None),
        P("expert", "dp", None),
    )
    return jax.shard_map(
        local, mesh=mesh, in_specs=placed, out_specs=P(("dp", "expert"), None), check_vma=False
    )
```

```python
import functools

import jax
import jax.numpy as jnp
from jax import lax
from jax.experimental import pallas as pl
from jax.experimental.pallas import tpu as pltpu
from jax.sharding import PartitionSpec as P

clamp_limit = 7.0
AXES = ("dp", "expert")
VMEM_LIMIT = 20 * 1024 * 1024
F32, BF16 = jnp.float32, jnp.bfloat16
PARAMS = {'far': [2, 6, 4, 3, 5, 7],
 'far_in': 2,
 'far_out': 3,
 'first': [0, 1, 2],
 'kcost': 0,
 'late': 2,
 'near_in': 1,
 'plan': [('out', 0),
          ('out', 1),
          ('out', 2),
          ('out', 6),
          ('back', 2),
          ('out', 4),
          ('back', 6),
          ('out', 3),
          ('back', 4),
          ('out', 5),
          ('back', 3),
          ('out', 7),
          ('back', 5),
          ('back', 7),
          ('back', 1),
          ('back', 0)],
 'ties': {'copy': (('out', 0),),
          'dn': (('out', 0), ('z', 1), ('z', 2)),
          'gu': (('out', 0), ('z', 1), ('z', 2)),
          ('back', 1): (('r', 3),),
          ('back', 2): (('r', 1),),
          ('back', 5): (('r', 6),),
          ('back', 7): (('r', 4),),
          ('out', 5): (('r', 2),),
          ('out', 7): (('r', 7),)},
 'xdepth': 2}


def sent_to(array, target):
    dp_size, expert_size = lax.axis_size("dp"), lax.axis_size("expert")
    pairs = []
    for d in range(dp_size):
        for e in range(expert_size):
            td, te = target(d, e)
            pairs.append((d * expert_size + e, td * expert_size + te))
    return lax.ppermute(array, AXES, pairs)


def to_other_core(array):
    return sent_to(array, lambda d, e: (d ^ 1, e))


def to_chip(step):
    dp_size = lax.axis_size("dp")
    return lambda array: sent_to(array, lambda d, e: ((d + 2 * step) % dp_size, e))


def moved(e, k, groups, sign):
    return (e // 2 + sign * (k // 2)) % (groups // 2) * 2 + (e % 2 ^ k % 2)


def to_expert(k):
    return lambda array: sent_to(array, lambda d, e: (d, moved(e, k, lax.axis_size("expert"), 1)))


def from_expert(k):
    return lambda array: sent_to(array, lambda d, e: (d, moved(e, k, lax.axis_size("expert"), -1)))


def after(array, *others):
    return lax.optimization_barrier((array, others))[0] if others else array


class Line:
    def __init__(self, depth):
        self.depth = depth
        self.done = []

    def send(self, array, move, ties=()):
        if len(self.done) >= self.depth:
            ties = [*ties, self.done[-self.depth]]
        moved = move(after(array, *ties))
        self.done.append(moved)
        return moved


def call_kernel(body, out_shapes, args, flops, scratch=()):
    moved = sum(a.size * a.dtype.itemsize for a in args) + sum(s.size * s.dtype.itemsize for s in out_shapes)
    return pl.pallas_call(
        body,
        out_shape=out_shapes,
        in_specs=[pl.BlockSpec(memory_space=pltpu.VMEM)] * len(args),
        out_specs=[pl.BlockSpec(memory_space=pltpu.VMEM)] * len(out_shapes),
        scratch_shapes=[pltpu.VMEM(shape, F32) for shape in scratch],
        compiler_params=pltpu.CompilerParams(vmem_limit_bytes=VMEM_LIMIT),
        cost_estimate=pl.CostEstimate(flops=flops, bytes_accessed=moved, transcendentals=0),
    )(*args)


def packed_rows(capacity, width):
    tiles, rest = divmod(width, 128)
    assert rest * 2 <= 128
    first = -(-(-(-capacity // 2)) // 8) * 8
    return -(-(tiles * capacity + (first if rest else 0)) // 16) * 16, first


def pack(block, capacity, out_ref):
    rows, width = block.shape
    tiles, rest = divmod(width, 128)
    for t in range(tiles):
        out_ref[pl.ds(t * capacity, rows)] = block[:, t * 128 : (t + 1) * 128]
    if rest:
        first = packed_rows(capacity, width)[1]
        left, right = block[:first, tiles * 128 :], block[first:, tiles * 128 :]
        if rows - first < first:
            right = jnp.concatenate([right, jnp.zeros((2 * first - rows, rest), F32)], axis=0)
        parts = [left, right[:first]]
        if rest < 64:
            parts = [jnp.pad(p, ((0, 0), (0, 64 - rest))) for p in parts]
        out_ref[pl.ds(tiles * capacity, first)] = jnp.concatenate(parts, axis=1)


def unpack(packed_ref, capacity, rows, low, out_ref):
    width = out_ref.shape[1]
    tiles, rest = divmod(width, 128)
    for t in range(tiles):
        out_ref[low : low + rows, t * 128 : (t + 1) * 128] = packed_ref[pl.ds(t * capacity, rows)]
    if rest:
        first = packed_rows(capacity, width)[1]
        tail = packed_ref[pl.ds(tiles * capacity, first)]
        out_ref[low : low + first, tiles * 128 :] = tail[:, :rest]
        out_ref[low + first : low + rows, tiles * 128 :] = tail[: rows - first, 64 : 64 + rest]


def pick_kernel(capacity, sel_ref, hid_ref, *refs):
    hid, scratch = hid_ref[...].T, refs[-1]
    for k, out_ref in enumerate(refs[:-1]):
        pack(jnp.dot(sel_ref[k], hid, preferred_element_type=F32), capacity, scratch)
        out_ref[...] = scratch[: out_ref.shape[0]].astype(BF16)


def expert_kernel(capacity, blocks, shards, *refs):
    row_refs, up_refs, down_refs = refs[:blocks], refs[blocks : blocks + shards], refs[blocks + shards : blocks + 2 * shards]
    out_refs, packed, spread = refs[blocks + 2 * shards : -2], refs[-2], refs[-1]
    slots = spread.shape[0] // blocks
    for s, ref in enumerate(row_refs):
        packed[: ref.shape[0]] = ref[...].astype(F32)
        unpack(packed, capacity, slots, s * slots, spread)
    rows = spread[...].astype(BF16)
    dims = (((1,), (1,)), ((), ()))
    total = None
    for up_ref, down_ref in zip(up_refs, down_refs):
        gate = lax.dot_general(rows, up_ref[0], dims, preferred_element_type=F32)
        upper = lax.dot_general(rows, up_ref[1], dims, preferred_element_type=F32)
        gate = jnp.minimum(gate, clamp_limit)
        upper = jnp.clip(upper, -clamp_limit, clamp_limit)
        hidden = ((upper + 1.0) * gate * jax.nn.sigmoid(1.702 * gate)).astype(BF16)
        part = jnp.dot(hidden, down_ref[...], preferred_element_type=F32)
        total = part if total is None else total + part
    for s, out_ref in enumerate(out_refs):
        pack(total[s * slots : (s + 1) * slots], capacity, packed)
        out_ref[...] = packed[: out_ref.shape[0]].astype(out_ref.dtype)


def add_kernel(*refs):
    total = refs[0][...]
    for ref in refs[1:-1]:
        total += ref[...].astype(F32)
    refs[-1][...] = total.astype(BF16)


def combine_kernel(capacity, final, blocks, table_ref, *refs):
    out_ref, packed, spread = refs[-3:]
    total = None
    for k in range(blocks):
        packed[: refs[k].shape[0]] = refs[k][...].astype(F32)
        unpack(packed, capacity, spread.shape[0], 0, spread)
        part = jnp.dot(table_ref[k], spread[...].astype(BF16), preferred_element_type=F32)
        total = part if total is None else total + part
    for ref in refs[blocks:-3]:
        total += ref[...]
    out_ref[...] = total.T.astype(BF16) if final else total


def general_plan(groups):
    return [step for k in range(groups) for step in (("out", k), ("back", k))]


def local(hidden_states, route_ids, route_weights, gate_up_proj, down_proj):
    tok_rows, width = hidden_states.shape
    top_count = route_ids.shape[1]
    units = gate_up_proj.shape[1]
    groups = lax.axis_size("expert")
    chips = lax.axis_size("dp") // 2
    capacity = max(2, 17 * tok_rows * top_count // (16 * groups))
    slots = -(-capacity // 8) * 8
    packed = (packed_rows(capacity, width)[0], 128)
    packed_scratch = (packed[0] + slots, 128)
    half = groups // 2
    me = lax.axis_index("expert")
    known = groups == 8 and chips == 2
    steps = PARAMS["plan"] if known else general_plan(groups)
    tied = PARAMS["ties"] if known else {}
    far_order = PARAMS["far"] if known else list(range(2, groups))

    relative = lax.rem(route_ids // 2 - me // 2 + half, half) * 2 + ((route_ids ^ me) & 1)
    near = relative[:, :, None] == jnp.arange(groups, dtype=jnp.int32)
    member = jnp.any(near, axis=1)
    weight = jnp.sum(jnp.where(near, route_weights[:, :, None].astype(F32), 0.0), axis=1)
    before = jnp.tril(jnp.ones((tok_rows, tok_rows), BF16), -1)
    rank = jnp.dot(before, member.astype(BF16), preferred_element_type=F32).astype(jnp.int32)
    rank = jnp.where(member, rank, -1)
    slot_range = jnp.arange(slots, dtype=jnp.int32)
    chosen = rank.T[:, None, :] == slot_range[None, :, None]
    table = jnp.where(rank.T[:, :, None] == slot_range, weight.T[:, :, None], 0.0).astype(BF16)
    outgoing = [None] * groups
    first = PARAMS["first"] if known else list(range(groups))
    for blocks in (first, [k for k in range(groups) if k not in first]):
        if blocks:
            picked = call_kernel(
                functools.partial(pick_kernel, capacity),
                [jax.ShapeDtypeStruct(packed, BF16)] * len(blocks),
                (jnp.stack([chosen[k] for k in blocks]).astype(BF16), hidden_states.T),
                2 * len(blocks) * slots * tok_rows * width,
                [packed_scratch],
            )
            for k, block in zip(blocks, picked):
                outgoing[k] = block
    between_chips, far_in = Line(PARAMS["xdepth"] * (chips - 1)), Line(PARAMS["far_in"])
    near_in, far_out, near_out = Line(PARAMS["near_in"]), Line(PARAMS["far_out"]), Line(1)
    done, rows = {}, [outgoing[0]] + [None] * (groups - 1)

    def ties_of(name):
        return [done[t] for t in tied.get(name, ()) if t in done]

    for k in far_order:
        rows[k] = done["z", k] = far_in.send(outgoing[k], to_expert(k), ties_of(("z", k)))
    rows[1] = done["z", 1] = near_in.send(outgoing[1], to_expert(1), ties_of(("z", 1)))
    partial, results, weights = {}, [None] * groups, None
    for what, k in steps:
        name = (what, k)
        if what == "out":
            if rows[k] is None:
                rows[k] = done["z", k] = near_in.send(outgoing[k], to_expert(k), ties_of(("z", k)))
            others = [between_chips.send(rows[k], to_chip(s), ties_of(name)) for s in range(1, chips)]
            done[name] = others[0]
            if weights is None:
                own_gu = jnp.transpose(after(gate_up_proj[0], *ties_of("copy")), (1, 0, 2))
                core_gu = done["gu"] = to_other_core(after(own_gu, *ties_of("gu")))
                core_dn = done["dn"] = to_other_core(after(down_proj[0], *ties_of("dn")))
                weights = [own_gu, core_gu, down_proj[0], core_dn]
            partial[k] = call_kernel(
                functools.partial(expert_kernel, capacity, chips, 2),
                [jax.ShapeDtypeStruct(packed, F32)] + [jax.ShapeDtypeStruct(packed, BF16)] * (chips - 1),
                (rows[k], *others, *weights),
                PARAMS["kcost"] * chips * slots * width * 2 * units,
                [packed_scratch, (chips * slots, width)],
            )
            continue
        mine, *foreign = partial[k]
        back = [between_chips.send(v, to_chip(-s), ties_of(name)) for s, v in enumerate(foreign, 1)]
        done[name] = back[0]
        out, = call_kernel(add_kernel, [jax.ShapeDtypeStruct(packed, BF16)], (mine, *back), 0)
        line = far_out if k >= 2 else near_out
        results[k] = done["r", k] = line.send(out, from_expert(k), ties_of(("r", k))) if k else out
    order, sums = [k for what, k in steps if what == "back"], ()
    late = min(PARAMS["late"], groups)
    for first, last in ((0, groups - late), (groups - late, groups)):
        blocks, final = order[first:last], last == groups
        if blocks:
            shape = jax.ShapeDtypeStruct((width, tok_rows), BF16) if final else jax.ShapeDtypeStruct((tok_rows, width), F32)
            sums = call_kernel(
                functools.partial(combine_kernel, capacity, final, len(blocks)),
                [shape],
                (jnp.stack([table[k] for k in blocks]), *[results[k] for k in blocks], *sums),
                2 * len(blocks) * slots * tok_rows * width,
                [packed_scratch, (slots, width)],
            )
    return sums[0].T


def solution(mesh):
    placed = (
        P(("dp", "expert"), None),
        P(("dp", "expert"), None),
        P(("dp", "expert"), None),
        P("expert", "dp", None, None),
        P("expert", "dp", None),
    )
    return jax.shard_map(
        local, mesh=mesh, in_specs=placed, out_specs=P(("dp", "expert"), None), check_vma=False
    )
```

```python
import functools

import jax
import jax.numpy as jnp
from jax import lax
from jax.experimental import pallas as pl
from jax.experimental.pallas import tpu as pltpu
from jax.sharding import PartitionSpec as P

clamp_limit = 7.0
AXES = ("dp", "expert")
VMEM_LIMIT = 20 * 1024 * 1024
F32, BF16 = jnp.float32, jnp.bfloat16
PARAMS = {'far': [2, 6, 4, 3, 5, 7],
 'far_in': 2,
 'far_out': 3,
 'first': [0, 1, 2],
 'kcost': 0,
 'late': 2,
 'near_in': 1,
 'plan': [('out', 0),
          ('out', 1),
          ('out', 2),
          ('out', 6),
          ('back', 2),
          ('out', 4),
          ('back', 6),
          ('out', 3),
          ('back', 4),
          ('out', 5),
          ('back', 3),
          ('out', 7),
          ('back', 5),
          ('back', 7),
          ('back', 1),
          ('back', 0)],
 'ties': {'copy': (('out', 0),),
          'dn': (('out', 0), ('z', 1), ('z', 2)),
          'gu': (('out', 0), ('z', 1), ('z', 2)),
          ('back', 1): (('r', 3),),
          ('back', 2): (('r', 1),),
          ('back', 4): (('z', 6),),
          ('back', 5): (('r', 6), ('z', 7)),
          ('back', 7): (('r', 4),),
          ('out', 1): (('r', 7),),
          ('out', 5): (('r', 2),),
          ('out', 7): (('r', 7),)},
 'xdepth': 2}


def sent_to(array, target):
    dp_size, expert_size = lax.axis_size("dp"), lax.axis_size("expert")
    pairs = []
    for d in range(dp_size):
        for e in range(expert_size):
            td, te = target(d, e)
            pairs.append((d * expert_size + e, td * expert_size + te))
    return lax.ppermute(array, AXES, pairs)


def to_other_core(array):
    return sent_to(array, lambda d, e: (d ^ 1, e))


def to_chip(step):
    dp_size = lax.axis_size("dp")
    return lambda array: sent_to(array, lambda d, e: ((d + 2 * step) % dp_size, e))


def moved(e, k, groups, sign):
    return (e // 2 + sign * (k // 2)) % (groups // 2) * 2 + (e % 2 ^ k % 2)


def to_expert(k):
    return lambda array: sent_to(array, lambda d, e: (d, moved(e, k, lax.axis_size("expert"), 1)))


def from_expert(k):
    return lambda array: sent_to(array, lambda d, e: (d, moved(e, k, lax.axis_size("expert"), -1)))


def after(array, *others):
    return lax.optimization_barrier((array, others))[0] if others else array


class Line:
    def __init__(self, depth):
        self.depth = depth
        self.done = []

    def send(self, array, move, ties=()):
        if len(self.done) >= self.depth:
            ties = [*ties, self.done[-self.depth]]
        moved = move(after(array, *ties))
        self.done.append(moved)
        return moved


def call_kernel(body, out_shapes, args, flops, scratch=()):
    moved = sum(a.size * a.dtype.itemsize for a in args) + sum(s.size * s.dtype.itemsize for s in out_shapes)
    return pl.pallas_call(
        body,
        out_shape=out_shapes,
        in_specs=[pl.BlockSpec(memory_space=pltpu.VMEM)] * len(args),
        out_specs=[pl.BlockSpec(memory_space=pltpu.VMEM)] * len(out_shapes),
        scratch_shapes=[pltpu.VMEM(shape, F32) for shape in scratch],
        compiler_params=pltpu.CompilerParams(vmem_limit_bytes=VMEM_LIMIT),
        cost_estimate=pl.CostEstimate(flops=flops, bytes_accessed=moved, transcendentals=0),
    )(*args)


def packed_rows(capacity, width):
    tiles, rest = divmod(width, 128)
    assert rest * 2 <= 128
    first = -(-(-(-capacity // 2)) // 8) * 8
    return -(-(tiles * capacity + (first if rest else 0)) // 16) * 16, first


def pack(block, capacity, out_ref):
    rows, width = block.shape
    tiles, rest = divmod(width, 128)
    for t in range(tiles):
        out_ref[pl.ds(t * capacity, rows)] = block[:, t * 128 : (t + 1) * 128]
    if rest:
        first = packed_rows(capacity, width)[1]
        left, right = block[:first, tiles * 128 :], block[first:, tiles * 128 :]
        if rows - first < first:
            right = jnp.concatenate([right, jnp.zeros((2 * first - rows, rest), F32)], axis=0)
        parts = [left, right[:first]]
        if rest < 64:
            parts = [jnp.pad(p, ((0, 0), (0, 64 - rest))) for p in parts]
        out_ref[pl.ds(tiles * capacity, first)] = jnp.concatenate(parts, axis=1)


def unpack(packed_ref, capacity, rows, low, out_ref):
    width = out_ref.shape[1]
    tiles, rest = divmod(width, 128)
    for t in range(tiles):
        out_ref[low : low + rows, t * 128 : (t + 1) * 128] = packed_ref[pl.ds(t * capacity, rows)]
    if rest:
        first = packed_rows(capacity, width)[1]
        tail = packed_ref[pl.ds(tiles * capacity, first)]
        out_ref[low : low + first, tiles * 128 :] = tail[:, :rest]
        out_ref[low + first : low + rows, tiles * 128 :] = tail[: rows - first, 64 : 64 + rest]


def pick_kernel(capacity, sel_ref, hid_ref, *refs):
    hid, scratch = hid_ref[...].T, refs[-1]
    for k, out_ref in enumerate(refs[:-1]):
        pack(jnp.dot(sel_ref[k], hid, preferred_element_type=F32), capacity, scratch)
        out_ref[...] = scratch[: out_ref.shape[0]].astype(BF16)


def expert_kernel(capacity, blocks, shards, *refs):
    row_refs, up_refs, down_refs = refs[:blocks], refs[blocks : blocks + shards], refs[blocks + shards : blocks + 2 * shards]
    out_refs, packed, spread = refs[blocks + 2 * shards : -2], refs[-2], refs[-1]
    slots = spread.shape[0] // blocks
    for s, ref in enumerate(row_refs):
        packed[: ref.shape[0]] = ref[...].astype(F32)
        unpack(packed, capacity, slots, s * slots, spread)
    rows = spread[...].astype(BF16)
    dims = (((1,), (1,)), ((), ()))
    total = None
    for up_ref, down_ref in zip(up_refs, down_refs):
        gate = lax.dot_general(rows, up_ref[0], dims, preferred_element_type=F32)
        upper = lax.dot_general(rows, up_ref[1], dims, preferred_element_type=F32)
        gate = jnp.minimum(gate, clamp_limit)
        upper = jnp.clip(upper, -clamp_limit, clamp_limit)
        hidden = ((upper + 1.0) * gate * jax.nn.sigmoid(1.702 * gate)).astype(BF16)
        part = jnp.dot(hidden, down_ref[...], preferred_element_type=F32)
        total = part if total is None else total + part
    for s, out_ref in enumerate(out_refs):
        pack(total[s * slots : (s + 1) * slots], capacity, packed)
        out_ref[...] = packed[: out_ref.shape[0]].astype(out_ref.dtype)


def add_kernel(*refs):
    total = refs[0][...]
    for ref in refs[1:-1]:
        total += ref[...].astype(F32)
    refs[-1][...] = total.astype(BF16)


def combine_kernel(capacity, final, blocks, table_ref, *refs):
    out_ref, packed, spread = refs[-3:]
    total = None
    for k in range(blocks):
        packed[: refs[k].shape[0]] = refs[k][...].astype(F32)
        unpack(packed, capacity, spread.shape[0], 0, spread)
        part = jnp.dot(table_ref[k], spread[...].astype(BF16), preferred_element_type=F32)
        total = part if total is None else total + part
    for ref in refs[blocks:-3]:
        total += ref[...]
    out_ref[...] = total.T.astype(BF16) if final else total


def general_plan(groups):
    return [step for k in range(groups) for step in (("out", k), ("back", k))]


def local(hidden_states, route_ids, route_weights, gate_up_proj, down_proj):
    tok_rows, width = hidden_states.shape
    top_count = route_ids.shape[1]
    units = gate_up_proj.shape[1]
    groups = lax.axis_size("expert")
    chips = lax.axis_size("dp") // 2
    capacity = max(2, 17 * tok_rows * top_count // (16 * groups))
    slots = -(-capacity // 8) * 8
    packed = (packed_rows(capacity, width)[0], 128)
    packed_scratch = (packed[0] + slots, 128)
    half = groups // 2
    me = lax.axis_index("expert")
    known = groups == 8 and chips == 2
    steps = PARAMS["plan"] if known else general_plan(groups)
    tied = PARAMS["ties"] if known else {}
    far_order = PARAMS["far"] if known else list(range(2, groups))

    relative = lax.rem(route_ids // 2 - me // 2 + half, half) * 2 + ((route_ids ^ me) & 1)
    near = relative[:, :, None] == jnp.arange(groups, dtype=jnp.int32)
    member = jnp.any(near, axis=1)
    weight = jnp.sum(jnp.where(near, route_weights[:, :, None].astype(F32), 0.0), axis=1)
    before = jnp.tril(jnp.ones((tok_rows, tok_rows), BF16), -1)
    rank = jnp.dot(before, member.astype(BF16), preferred_element_type=F32).astype(jnp.int32)
    rank = jnp.where(member, rank, -1)
    slot_range = jnp.arange(slots, dtype=jnp.int32)
    chosen = rank.T[:, None, :] == slot_range[None, :, None]
    table = jnp.where(rank.T[:, :, None] == slot_range, weight.T[:, :, None], 0.0).astype(BF16)
    outgoing = [None] * groups
    first = PARAMS["first"] if known else list(range(groups))
    for blocks in (first, [k for k in range(groups) if k not in first]):
        if blocks:
            picked = call_kernel(
                functools.partial(pick_kernel, capacity),
                [jax.ShapeDtypeStruct(packed, BF16)] * len(blocks),
                (jnp.stack([chosen[k] for k in blocks]).astype(BF16), hidden_states.T),
                2 * len(blocks) * slots * tok_rows * width,
                [packed_scratch],
            )
            for k, block in zip(blocks, picked):
                outgoing[k] = block
    between_chips, far_in = Line(PARAMS["xdepth"] * (chips - 1)), Line(PARAMS["far_in"])
    near_in, far_out, near_out = Line(PARAMS["near_in"]), Line(PARAMS["far_out"]), Line(1)
    done, rows = {}, [outgoing[0]] + [None] * (groups - 1)

    def ties_of(name):
        return [done[t] for t in tied.get(name, ()) if t in done]

    for k in far_order:
        rows[k] = done["z", k] = far_in.send(outgoing[k], to_expert(k), ties_of(("z", k)))
    rows[1] = done["z", 1] = near_in.send(outgoing[1], to_expert(1), ties_of(("z", 1)))
    partial, results, weights = {}, [None] * groups, None
    for what, k in steps:
        name = (what, k)
        if what == "out":
            if rows[k] is None:
                rows[k] = done["z", k] = near_in.send(outgoing[k], to_expert(k), ties_of(("z", k)))
            others = [between_chips.send(rows[k], to_chip(s), ties_of(name)) for s in range(1, chips)]
            done[name] = others[0]
            if weights is None:
                own_gu = jnp.transpose(after(gate_up_proj[0], *ties_of("copy")), (1, 0, 2))
                core_gu = done["gu"] = to_other_core(after(own_gu, *ties_of("gu")))
                core_dn = done["dn"] = to_other_core(after(down_proj[0], *ties_of("dn")))
                weights = [own_gu, core_gu, down_proj[0], core_dn]
            partial[k] = call_kernel(
                functools.partial(expert_kernel, capacity, chips, 2),
                [jax.ShapeDtypeStruct(packed, F32)] + [jax.ShapeDtypeStruct(packed, BF16)] * (chips - 1),
                (rows[k], *others, *weights),
                PARAMS["kcost"] * chips * slots * width * 2 * units,
                [packed_scratch, (chips * slots, width)],
            )
            continue
        mine, *foreign = partial[k]
        back = [between_chips.send(v, to_chip(-s), ties_of(name)) for s, v in enumerate(foreign, 1)]
        done[name] = back[0]
        out, = call_kernel(add_kernel, [jax.ShapeDtypeStruct(packed, BF16)], (mine, *back), 0)
        line = far_out if k >= 2 else near_out
        results[k] = done["r", k] = line.send(out, from_expert(k), ties_of(("r", k))) if k else out
    order, sums = [k for what, k in steps if what == "back"], ()
    late = min(PARAMS["late"], groups)
    for first, last in ((0, groups - late), (groups - late, groups)):
        blocks, final = order[first:last], last == groups
        if blocks:
            shape = jax.ShapeDtypeStruct((width, tok_rows), BF16) if final else jax.ShapeDtypeStruct((tok_rows, width), F32)
            sums = call_kernel(
                functools.partial(combine_kernel, capacity, final, len(blocks)),
                [shape],
                (jnp.stack([table[k] for k in blocks]), *[results[k] for k in blocks], *sums),
                2 * len(blocks) * slots * tok_rows * width,
                [packed_scratch, (slots, width)],
            )
    return sums[0].T


def solution(mesh):
    placed = (
        P(("dp", "expert"), None),
        P(("dp", "expert"), None),
        P(("dp", "expert"), None),
        P("expert", "dp", None, None),
        P("expert", "dp", None),
    )
    return jax.shard_map(
        local, mesh=mesh, in_specs=placed, out_specs=P(("dp", "expert"), None), check_vma=False
    )
```

```python
import functools

import jax
import jax.numpy as jnp
from jax import lax
from jax.experimental import pallas as pl
from jax.experimental.pallas import tpu as pltpu
from jax.sharding import PartitionSpec as P

clamp_limit = 7.0
AXES = ("dp", "expert")
VMEM_LIMIT = 14 * 1024 * 1024
F32, BF16 = jnp.float32, jnp.bfloat16
PARAMS = {'far': [2, 6, 4, 3, 5, 7],
 'far_in': 2,
 'far_out': 3,
 'first': [0, 1, 2],
 'kcost': 0,
 'late': 2,
 'near_in': 1,
 'plan': [('out', 0),
          ('out', 1),
          ('out', 2),
          ('out', 6),
          ('back', 2),
          ('out', 4),
          ('back', 6),
          ('out', 3),
          ('back', 4),
          ('out', 5),
          ('back', 3),
          ('out', 7),
          ('back', 5),
          ('back', 7),
          ('back', 1),
          ('back', 0)],
 'ties': {'copy': (('out', 0),),
          'dn': (('out', 0), ('z', 1), ('z', 2)),
          'gu': (('out', 0), ('z', 1), ('z', 2)),
          ('back', 1): (('r', 3),),
          ('back', 2): (('r', 1),),
          ('back', 4): (('z', 6),),
          ('back', 5): (('r', 6), ('z', 7)),
          ('back', 7): (('r', 4),),
          ('out', 1): (('r', 7),),
          ('out', 5): (('r', 2),),
          ('out', 7): (('r', 7),)},
 'xdepth': 2}


def sent_to(array, target):
    dp_size, expert_size = lax.axis_size("dp"), lax.axis_size("expert")
    pairs = []
    for d in range(dp_size):
        for e in range(expert_size):
            td, te = target(d, e)
            pairs.append((d * expert_size + e, td * expert_size + te))
    return lax.ppermute(array, AXES, pairs)


def to_other_core(array):
    return sent_to(array, lambda d, e: (d ^ 1, e))


def to_chip(step):
    dp_size = lax.axis_size("dp")
    return lambda array: sent_to(array, lambda d, e: ((d + 2 * step) % dp_size, e))


def moved(e, k, groups, sign):
    return (e // 2 + sign * (k // 2)) % (groups // 2) * 2 + (e % 2 ^ k % 2)


def to_expert(k):
    return lambda array: sent_to(array, lambda d, e: (d, moved(e, k, lax.axis_size("expert"), 1)))


def from_expert(k):
    return lambda array: sent_to(array, lambda d, e: (d, moved(e, k, lax.axis_size("expert"), -1)))


def after(array, *others):
    return lax.optimization_barrier((array, others))[0] if others else array


class Line:
    def __init__(self, depth):
        self.depth = depth
        self.done = []

    def send(self, array, move, ties=()):
        if len(self.done) >= self.depth:
            ties = [*ties, self.done[-self.depth]]
        moved = move(after(array, *ties))
        self.done.append(moved)
        return moved


def call_kernel(body, out_shapes, args, flops, scratch=()):
    moved = sum(a.size * a.dtype.itemsize for a in args) + sum(s.size * s.dtype.itemsize for s in out_shapes)
    return pl.pallas_call(
        body,
        out_shape=out_shapes,
        in_specs=[pl.BlockSpec(memory_space=pltpu.VMEM)] * len(args),
        out_specs=[pl.BlockSpec(memory_space=pltpu.VMEM)] * len(out_shapes),
        scratch_shapes=[pltpu.VMEM(shape, F32) for shape in scratch],
        compiler_params=pltpu.CompilerParams(vmem_limit_bytes=VMEM_LIMIT),
        cost_estimate=pl.CostEstimate(flops=flops, bytes_accessed=moved, transcendentals=0),
    )(*args)


def packed_rows(capacity, width):
    tiles, rest = divmod(width, 128)
    assert rest * 2 <= 128
    first = -(-(-(-capacity // 2)) // 8) * 8
    return -(-(tiles * capacity + (first if rest else 0)) // 16) * 16, first


def pack(block, capacity, out_ref):
    rows, width = block.shape
    tiles, rest = divmod(width, 128)
    for t in range(tiles):
        out_ref[pl.ds(t * capacity, rows)] = block[:, t * 128 : (t + 1) * 128]
    if rest:
        first = packed_rows(capacity, width)[1]
        left, right = block[:first, tiles * 128 :], block[first:, tiles * 128 :]
        if rows - first < first:
            right = jnp.concatenate([right, jnp.zeros((2 * first - rows, rest), F32)], axis=0)
        parts = [left, right[:first]]
        if rest < 64:
            parts = [jnp.pad(p, ((0, 0), (0, 64 - rest))) for p in parts]
        out_ref[pl.ds(tiles * capacity, first)] = jnp.concatenate(parts, axis=1)


def unpack(packed_ref, capacity, rows, low, out_ref):
    width = out_ref.shape[1]
    tiles, rest = divmod(width, 128)
    for t in range(tiles):
        out_ref[low : low + rows, t * 128 : (t + 1) * 128] = packed_ref[pl.ds(t * capacity, rows)]
    if rest:
        first = packed_rows(capacity, width)[1]
        tail = packed_ref[pl.ds(tiles * capacity, first)]
        out_ref[low : low + first, tiles * 128 :] = tail[:, :rest]
        out_ref[low + first : low + rows, tiles * 128 :] = tail[: rows - first, 64 : 64 + rest]


def pick_kernel(capacity, sel_ref, hid_ref, *refs):
    hid, scratch = hid_ref[...].T, refs[-1]
    for k, out_ref in enumerate(refs[:-1]):
        pack(jnp.dot(sel_ref[k], hid, preferred_element_type=F32), capacity, scratch)
        out_ref[...] = scratch[: out_ref.shape[0]].astype(BF16)


def expert_kernel(capacity, blocks, shards, *refs):
    row_refs, up_refs, down_refs = refs[:blocks], refs[blocks : blocks + shards], refs[blocks + shards : blocks + 2 * shards]
    out_refs, packed, spread = refs[blocks + 2 * shards : -2], refs[-2], refs[-1]
    slots = spread.shape[0] // blocks
    for s, ref in enumerate(row_refs):
        packed[: ref.shape[0]] = ref[...].astype(F32)
        unpack(packed, capacity, slots, s * slots, spread)
    rows = spread[...].astype(BF16)
    dims = (((1,), (1,)), ((), ()))
    total = None
    for up_ref, down_ref in zip(up_refs, down_refs):
        gate = lax.dot_general(rows, up_ref[0], dims, preferred_element_type=F32)
        upper = lax.dot_general(rows, up_ref[1], dims, preferred_element_type=F32)
        gate = jnp.minimum(gate, clamp_limit)
        upper = jnp.clip(upper, -clamp_limit, clamp_limit)
        hidden = ((upper + 1.0) * gate * jax.nn.sigmoid(1.702 * gate)).astype(BF16)
        part = jnp.dot(hidden, down_ref[...], preferred_element_type=F32)
        total = part if total is None else total + part
    for s, out_ref in enumerate(out_refs):
        pack(total[s * slots : (s + 1) * slots], capacity, packed)
        out_ref[...] = packed[: out_ref.shape[0]].astype(out_ref.dtype)


def add_kernel(*refs):
    total = refs[0][...]
    for ref in refs[1:-1]:
        total += ref[...].astype(F32)
    refs[-1][...] = total.astype(BF16)


def combine_kernel(capacity, final, blocks, table_ref, *refs):
    out_ref, packed, spread = refs[-3:]
    total = None
    for k in range(blocks):
        packed[: refs[k].shape[0]] = refs[k][...].astype(F32)
        unpack(packed, capacity, spread.shape[0], 0, spread)
        part = jnp.dot(table_ref[k], spread[...].astype(BF16), preferred_element_type=F32)
        total = part if total is None else total + part
    for ref in refs[blocks:-3]:
        total += ref[...]
    out_ref[...] = total.T.astype(BF16) if final else total


def general_plan(groups):
    return [step for k in range(groups) for step in (("out", k), ("back", k))]


def local(hidden_states, route_ids, route_weights, gate_up_proj, down_proj):
    tok_rows, width = hidden_states.shape
    top_count = route_ids.shape[1]
    units = gate_up_proj.shape[1]
    groups = lax.axis_size("expert")
    chips = lax.axis_size("dp") // 2
    capacity = max(2, 17 * tok_rows * top_count // (16 * groups))
    slots = -(-capacity // 8) * 8
    packed = (packed_rows(capacity, width)[0], 128)
    packed_scratch = (packed[0] + slots, 128)
    half = groups // 2
    me = lax.axis_index("expert")
    known = groups == 8 and chips == 2
    steps = PARAMS["plan"] if known else general_plan(groups)
    tied = PARAMS["ties"] if known else {}
    far_order = PARAMS["far"] if known else list(range(2, groups))

    relative = lax.rem(route_ids // 2 - me // 2 + half, half) * 2 + ((route_ids ^ me) & 1)
    near = relative[:, :, None] == jnp.arange(groups, dtype=jnp.int32)
    member = jnp.any(near, axis=1)
    weight = jnp.sum(jnp.where(near, route_weights[:, :, None].astype(F32), 0.0), axis=1)
    before = jnp.tril(jnp.ones((tok_rows, tok_rows), BF16), -1)
    rank = jnp.dot(before, member.astype(BF16), preferred_element_type=F32).astype(jnp.int32)
    rank = jnp.where(member, rank, -1)
    slot_range = jnp.arange(slots, dtype=jnp.int32)
    chosen = rank.T[:, None, :] == slot_range[None, :, None]
    table = jnp.where(rank.T[:, :, None] == slot_range, weight.T[:, :, None], 0.0).astype(BF16)
    outgoing = [None] * groups
    first = PARAMS["first"] if known else list(range(groups))
    for blocks in (first, [k for k in range(groups) if k not in first]):
        if blocks:
            picked = call_kernel(
                functools.partial(pick_kernel, capacity),
                [jax.ShapeDtypeStruct(packed, BF16)] * len(blocks),
                (jnp.stack([chosen[k] for k in blocks]).astype(BF16), hidden_states.T),
                2 * len(blocks) * slots * tok_rows * width,
                [packed_scratch],
            )
            for k, block in zip(blocks, picked):
                outgoing[k] = block
    between_chips, far_in = Line(PARAMS["xdepth"] * (chips - 1)), Line(PARAMS["far_in"])
    near_in, far_out, near_out = Line(PARAMS["near_in"]), Line(PARAMS["far_out"]), Line(1)
    done, rows = {}, [outgoing[0]] + [None] * (groups - 1)

    def ties_of(name):
        return [done[t] for t in tied.get(name, ()) if t in done]

    for k in far_order:
        rows[k] = done["z", k] = far_in.send(outgoing[k], to_expert(k), ties_of(("z", k)))
    rows[1] = done["z", 1] = near_in.send(outgoing[1], to_expert(1), ties_of(("z", 1)))
    partial, results, weights = {}, [None] * groups, None
    for what, k in steps:
        name = (what, k)
        if what == "out":
            if rows[k] is None:
                rows[k] = done["z", k] = near_in.send(outgoing[k], to_expert(k), ties_of(("z", k)))
            others = [between_chips.send(rows[k], to_chip(s), ties_of(name)) for s in range(1, chips)]
            done[name] = others[0]
            if weights is None:
                own_gu = jnp.transpose(after(gate_up_proj[0], *ties_of("copy")), (1, 0, 2))
                core_gu = done["gu"] = to_other_core(after(own_gu, *ties_of("gu")))
                core_dn = done["dn"] = to_other_core(after(down_proj[0], *ties_of("dn")))
                weights = [own_gu, core_gu, down_proj[0], core_dn]
            partial[k] = call_kernel(
                functools.partial(expert_kernel, capacity, chips, 2),
                [jax.ShapeDtypeStruct(packed, F32)] + [jax.ShapeDtypeStruct(packed, BF16)] * (chips - 1),
                (rows[k], *others, *weights),
                PARAMS["kcost"] * chips * slots * width * 2 * units,
                [packed_scratch, (chips * slots, width)],
            )
            continue
        mine, *foreign = partial[k]
        back = [between_chips.send(v, to_chip(-s), ties_of(name)) for s, v in enumerate(foreign, 1)]
        done[name] = back[0]
        out, = call_kernel(add_kernel, [jax.ShapeDtypeStruct(packed, BF16)], (mine, *back), 0)
        line = far_out if k >= 2 else near_out
        results[k] = done["r", k] = line.send(out, from_expert(k), ties_of(("r", k))) if k else out
    order, sums = [k for what, k in steps if what == "back"], ()
    late = min(PARAMS["late"], groups)
    for first, last in ((0, groups - late), (groups - late, groups)):
        blocks, final = order[first:last], last == groups
        if blocks:
            shape = jax.ShapeDtypeStruct((width, tok_rows), BF16) if final else jax.ShapeDtypeStruct((tok_rows, width), F32)
            sums = call_kernel(
                functools.partial(combine_kernel, capacity, final, len(blocks)),
                [shape],
                (jnp.stack([table[k] for k in blocks]), *[results[k] for k in blocks], *sums),
                2 * len(blocks) * slots * tok_rows * width,
                [packed_scratch, (slots, width)],
            )
    return sums[0].T


def solution(mesh):
    placed = (
        P(("dp", "expert"), None),
        P(("dp", "expert"), None),
        P(("dp", "expert"), None),
        P("expert", "dp", None, None),
        P("expert", "dp", None),
    )
    return jax.shard_map(
        local, mesh=mesh, in_specs=placed, out_specs=P(("dp", "expert"), None), check_vma=False
    )
```
